32 devices in a mesh: blk: 32 (over z, y, x, core).
Axes of the slice: x: 2, y: 2, z: 4, core: 2. Of those that a mesh axis runs over, the one named last changes fastest.
Arguments:
- hidden: bfloat16 [64, 2048], P('blk')
- norm_gain: float32 [2048], replicated, may hold values from 0.5 to 1.5
- head_weight: bfloat16 [102400, 2048], P('blk')
- targets: int32 [64], P('blk'), may hold values from 0 to 102399
- spans: int32 [32, 2], P('blk'), may hold values from 0 to 2, as said below
Outputs:
- logprob: float32 [64], P('blk')
- entropy: float32 [64], P('blk')
The draws below stay inside these ranges and needn't reach their ends.
Inputs may be any that keep to these rules, and one draw needn't show every extreme that they name: 0 <= spans[k, 0] < spans[k, 1] <= 2; some device has the whole piece scored.
All inputs are finite; a program needn't handle non-finite values.
Results may differ from the reference program's by a relative error of at most 0.00073.
Values may be sent and summed in bfloat16 or wider, within the bound.
A program may use at most 64 MiB of HBM per device.

```python
import math
import jax
import jax.numpy as jnp
import numpy as np
from jax import lax

D = 2048
V = 102400
CAP = 2
HOLDERS = 32
ROWS = 64


def draw_hidden(key, part):
    noise_key = jax.random.fold_in(key, 11)
    key_one, key_two, key_three = jax.random.split(noise_key, 3)
    row_scale = jnp.exp(jax.random.uniform(key_two, (ROWS, 1), jnp.float32, 0.0, jnp.log(10.0)))
    col_scale = jnp.exp(jax.random.uniform(key_three, (1, D), jnp.float32, jnp.log(0.3), jnp.log(3.0)))
    noise_base = jax.random.normal(key_one, (ROWS, D), jnp.float32)
    values = noise_base * row_scale * col_scale
    return values.astype(jnp.bfloat16)


def draw_head_weight(key, part):
    noise_key = jax.random.fold_in(key, 13)
    scale_head = 3.0 / D ** 0.5
    values = jax.random.normal(noise_key, (V, D), jnp.float32) * scale_head
    return values.astype(jnp.bfloat16)


def draw_spans(key, part):
    key_one, key_two, key_three = jax.random.split(jax.random.fold_in(key, 17), 3)
    middle = CAP // 2
    first = jax.random.randint(key_one, (HOLDERS,), 0, middle + 1)
    last = jax.random.randint(key_two, (HOLDERS,), middle + 1, CAP + 1)
    chosen = jax.random.randint(key_three, (), 0, HOLDERS)
    holder_ids = jnp.arange(HOLDERS)
    first = jnp.where(holder_ids == chosen, 0, first)
    last = jnp.where(holder_ids == chosen, CAP, last)
    return jnp.stack([first, last], axis=1).astype(jnp.int32)


def with_ends(values, stream_key, smallest, top_value):
    dims = values.shape
    spot = [jax.random.randint(jax.random.fold_in(stream_key, axis), (), 0, dims[axis]) for axis in range(len(dims))]
    values = values.at[tuple(spot)].set(smallest)
    longest = dims.index(max(dims))
    spot[longest] = (spot[longest] + 1) % dims[longest]
    return values.at[tuple(spot)].set(top_value)


def ranked_wide(key, dims, amount, slope):
    weights = [min(1 << octave, amount + 1 - (1 << octave)) * (1 << 20) // math.isqrt((1 << octave) ** slope) + 1 for octave in range((amount + 1).bit_length()) if 1 << octave <= amount]
    deviation = 1 + sum(weights) // (1 << 30)
    listing = np.cumsum(np.array([max(1, weight // deviation) for weight in weights]))
    ticket = jax.random.randint(jax.random.fold_in(key, 1), dims, 0, int(listing[len(weights) - 1]))
    start = jnp.left_shift(1, jnp.searchsorted(jnp.asarray(listing, jnp.int32), ticket, side="right").astype(jnp.int32))
    standing = start - 1 + jax.random.randint(jax.random.fold_in(key, 4), dims, 0, 1 << 30) % jnp.minimum(start, amount + 1 - start)
    return jax.random.permutation(jax.random.fold_in(key, 2), amount)[standing].astype(jnp.int32)


def setup_inputs(seed: int = 0) -> dict:
    keys = jax.random.split(jax.random.key(seed), 6)
    hidden = draw_hidden(jax.random.fold_in(keys[5], 71), 0)
    norm_gain = jnp.clip(1.0 + 0.1 * jax.random.normal(keys[1], (D,), jnp.float32), 0.5, 1.5)
    head_weight = draw_head_weight(jax.random.fold_in(keys[5], 71), 0)
    targets = with_ends(ranked_wide(keys[3], (ROWS,), V, 2), jax.random.fold_in(keys[3], 3), 0, V - 1).astype(jnp.int32)
    spans = draw_spans(jax.random.fold_in(keys[5], 71), 0)
    return dict(hidden=hidden, norm_gain=norm_gain, head_weight=head_weight, targets=targets, spans=spans)


epsilon = 1e-06

def combine(first, second):
    peak = jnp.maximum(first[0], second[0])
    scale_one = jnp.exp(first[0] - peak)
    scale_two = jnp.exp(second[0] - peak)
    return (peak, first[1] * scale_one + second[1] * scale_two, first[2] * scale_one + second[2] * scale_two, first[3] + second[3])

def reference(hidden, norm_gain, head_weight, targets, spans):
    values = hidden.astype(jnp.float32)
    meansq = lax.optimization_barrier(jnp.mean(values * values, axis=-1, keepdims=True))
    normed = (values * lax.rsqrt(meansq + epsilon) * norm_gain.astype(jnp.float32)).astype(jnp.bfloat16)
    width = V // 16

    def one_block(carry, block_index):
        vocab_rows = lax.dynamic_slice_in_dim(head_weight, block_index * width, width, 0)
        logits = jnp.dot(normed, vocab_rows.T, preferred_element_type=jnp.float32)
        peak = lax.optimization_barrier(jnp.max(logits, axis=-1))
        expon = jnp.exp(logits - peak[:, None])
        col_ids = block_index * width + jnp.arange(width, dtype=jnp.int32)
        picked = lax.optimization_barrier(jnp.sum(jnp.where(col_ids[None, :] == targets[:, None], logits, jnp.float32(0.0)), axis=-1))
        fresh = (peak, lax.optimization_barrier(jnp.sum(expon, axis=-1)), lax.optimization_barrier(jnp.sum(expon * logits, axis=-1)), picked)
        return (combine(carry, fresh), None)
    start_state = (jnp.full((ROWS,), -jnp.inf, jnp.float32), jnp.zeros((ROWS,), jnp.float32), jnp.zeros((ROWS,), jnp.float32), jnp.zeros((ROWS,), jnp.float32))
    final, _ = lax.scan(one_block, start_state, jnp.arange(16, dtype=jnp.int32))
    lse = final[0] + jnp.log(final[1])
    expected = final[2] / final[1]
    row_ids = jnp.arange(ROWS, dtype=jnp.int32)
    slot_ids = row_ids % CAP
    holder = row_ids // CAP
    scored = (slot_ids >= spans[holder, 0]) & (slot_ids < spans[holder, 1])
    logprob = jnp.where(scored, final[3] - lse, jnp.float32(0.0))
    entropy = jnp.where(scored, lse - expected, jnp.float32(0.0))
    return (logprob, entropy)
```

```python
import functools

import jax
import jax.numpy as jnp
from jax import lax
from jax.experimental import pallas as pl
from jax.experimental.pallas import tpu as pltpu
from jax.sharding import PartitionSpec as P

epsilon = 1e-06
MESH = pl.DeviceIdType.MESH


def largest_block(count, limit, step):
    sizes = [size for size in range(step, min(count, limit) + 1, step) if count % size == 0]
    return max(sizes) if sizes else count


def split_of(n):
    cores = 2 if n % 2 == 0 else 1
    plane = 4 if n % (cores * 4) == 0 else 1
    return n // (cores * plane), plane, cores


def kernel(
    n, blocks, hidden_ref, gain_ref, weight_ref, targets_ref, spans_ref, logprob_ref, entropy_ref,
    hid, gain, weight, rows, wide, operand, logits, own_targets, all_targets, message,
    inbox, load_sem, weight_sem, row_send, row_recv, target_send, target_recv, stat_send, stat_recv,
):
    me = lax.axis_index("blk")
    slots, width = hid.shape
    chunks = width // 128
    piece = slots * chunks
    row_count = n * slots
    block = weight.shape[0] // blocks
    high_size, plane_size, core_size = split_of(n)

    loads = [
        pltpu.make_async_copy(hidden_ref, hid, load_sem.at[0]),
        pltpu.make_async_copy(gain_ref, gain, load_sem.at[1]),
    ]
    for load in loads:
        load.start()

    def weight_copy(index):
        where = pl.ds(index * block, block)
        return pltpu.make_async_copy(weight_ref.at[where], weight.at[where], weight_sem.at[index])

    for index in range(blocks):
        weight_copy(index).start()

    barrier = pltpu.get_barrier_semaphore()

    @pl.loop(1, n)
    def _(step):
        pl.semaphore_signal(barrier, inc=1, device_id=(lax.rem(me + step, n),), device_id_type=MESH)

    for load in loads:
        load.wait()

    values = hid[...].astype(jnp.float32)
    meansq = jnp.mean(values * values, axis=-1, keepdims=True)
    values = values * lax.rsqrt(meansq + epsilon)
    mine = wide.at[0]
    for chunk in range(chunks):
        mine[:, chunk, :] = values[:, chunk * 128 : (chunk + 1) * 128]
    start = pl.multiple_of(me * piece, piece)
    normed = (mine[...] * gain[...][None]).astype(jnp.bfloat16)
    rows[pl.ds(start, piece), :] = normed.reshape(piece, 128)

    lanes = lax.broadcasted_iota(jnp.int32, own_targets.shape, 1)
    spread = jnp.zeros(own_targets.shape, jnp.int32)
    for slot in range(slots):
        spread = jnp.where(lanes == slot * n + me, targets_ref[slot], spread)
    own_targets[...] = spread
    all_targets[me] = spread

    pl.semaphore_wait(barrier, n - 1)

    def index_of(high, plane, core):
        return (high * plane_size + plane) * core_size + core

    core = lax.rem(me, core_size)
    plane = lax.rem(me // core_size, plane_size)
    high = me // (core_size * plane_size)

    def row_copy(owner, device):
        where = pl.ds(pl.multiple_of(owner * piece, piece), piece)
        return pltpu.make_async_remote_copy(
            src_ref=rows.at[where],
            dst_ref=rows.at[where],
            send_sem=row_send,
            recv_sem=row_recv.at[owner],
            device_id=(device,),
            device_id_type=MESH,
        )

    def arrive(owner):
        row_copy(owner, me).wait_recv()

    def spread_plane(owner):
        for step in range(1, plane_size):
            row_copy(owner, index_of(high, lax.rem(plane + step, plane_size), core)).start()

    def spread_core(owner):
        for step in range(1, core_size):
            row_copy(owner, index_of(high, plane, lax.rem(core + step, core_size))).start()

    @pl.loop(1, high_size)
    def _(step):
        row_copy(me, index_of(lax.rem(high + step, high_size), plane, core)).start()

    spread_plane(me)
    spread_core(me)

    def target_copy(device):
        return pltpu.make_async_remote_copy(
            src_ref=own_targets,
            dst_ref=all_targets.at[me],
            send_sem=target_send,
            recv_sem=target_recv,
            device_id=(device,),
            device_id_type=MESH,
        )

    @pl.loop(1, high_size)
    def _(step):
        owner = index_of(lax.rem(high + step, high_size), plane, core)
        arrive(owner)
        spread_plane(owner)
        spread_core(owner)

    @pl.loop(0, high_size)
    def _(step):
        for other in range(1, plane_size):
            owner = index_of(
                lax.rem(high + step, high_size), lax.rem(plane + other, plane_size), core
            )
            arrive(owner)
            spread_core(owner)

    @pl.loop(1, n)
    def _(step):
        target_copy(lax.rem(me + step, n)).start()

    for other in range(1, core_size):

        @pl.loop(0, high_size)
        def _(step):
            for place in range(plane_size):
                arrive(index_of(step, place, lax.rem(core + other, core_size)))

    group = min(n, 32)

    @pl.loop(0, n // group)
    def _(index):
        first = pl.multiple_of(index * group * piece, group * piece)
        wide[...] = (
            rows[pl.ds(first, group * piece), :]
            .astype(jnp.float32)
            .reshape(group, slots, chunks, 128)
        )
        for slot in range(slots):
            place = pl.ds(pl.multiple_of(slot * n + index * group, group), group)
            for chunk in range(chunks):
                operand[place, chunk * 128 : (chunk + 1) * 128] = wide[:, slot, chunk, :].astype(
                    jnp.bfloat16
                )

    peak = None
    for index in range(blocks):
        weight_copy(index).wait()
        where = pl.ds(index * block, block)
        product = lax.dot_general(
            weight[where, :],
            operand[...],
            (((1,), (1,)), ((), ())),
            preferred_element_type=jnp.float32,
        )
        logits[where, :] = product
        top = jnp.max(product, axis=0, keepdims=True)
        peak = top if peak is None else jnp.maximum(peak, top)

    everyone = all_targets.at[pl.ds(0, n - 1)]
    pltpu.make_async_copy(everyone, everyone, target_recv).wait()
    wanted = jnp.sum(all_targets[...], axis=0)[:, :row_count] - me * weight.shape[0]
    found = logits[...]
    column = lax.broadcasted_iota(jnp.int32, found.shape, 0)
    expon = jnp.exp(found - peak)
    total = jnp.sum(expon, axis=0, keepdims=True)
    moment = jnp.sum(expon * found, axis=0, keepdims=True)
    picked = jnp.sum(jnp.where(column == wanted, found, 0.0), axis=0, keepdims=True)

    def by_slot(item):
        return [item[:, slot * n : (slot + 1) * n] for slot in range(slots)]

    blank = [jnp.zeros((1, n), jnp.float32)] * slots
    packed = jnp.concatenate(
        by_slot(total) + by_slot(moment) + by_slot(picked) + blank
        + by_slot(peak) + by_slot(peak) + blank + blank,
        axis=0,
    )
    turned = packed.T
    fields = turned.shape[1]
    turned = jnp.concatenate([turned, jnp.zeros((n, 128 - fields), jnp.float32)], axis=1)
    message[...] = turned.reshape(n, 1, 128)
    inbox[me] = message[me]

    def stat_copy(device):
        return pltpu.make_async_remote_copy(
            src_ref=message.at[device],
            dst_ref=inbox.at[me],
            send_sem=stat_send,
            recv_sem=stat_recv,
            device_id=(device,),
            device_id_type=MESH,
        )

    @pl.loop(1, n)
    def _(step):
        stat_copy(lax.rem(me + step, n)).start()

    others = inbox.at[pl.ds(0, n - 1)]
    pltpu.make_async_copy(others, others, stat_recv).wait()
    parts = inbox[...].reshape(n, 128)
    peaks = pltpu.roll(parts, 128 - fields // 2, 1)
    top = jnp.max(peaks, axis=0, keepdims=True)
    merged = jnp.sum(parts * jnp.exp(peaks - top), axis=0, keepdims=True)[:, :128]
    lse = top + jnp.log(merged)
    expected = pltpu.roll(merged, 128 - slots, 1) / merged
    chosen = pltpu.roll(merged, 128 - 2 * slots, 1)
    slot_ids = lax.broadcasted_iota(jnp.int32, (1, 128), 1)
    scored = (slot_ids >= spans_ref[0, 0]) & (slot_ids < spans_ref[0, 1])
    logprob_ref[...] = jnp.where(scored, chosen - lse, 0.0)[:, :slots]
    entropy_ref[...] = jnp.where(scored, lse - expected, 0.0)[:, :slots]

    sent = rows.at[pl.ds(0, (n - 1) * piece)]
    pltpu.make_async_copy(sent, sent, row_send).wait()
    pltpu.make_async_copy(everyone, everyone, target_send).wait()
    pltpu.make_async_copy(others, others, stat_send).wait()


def local(n, hidden, norm_gain, head_weight, targets, spans):
    slots, width = hidden.shape
    vocab = head_weight.shape[0]
    chunks = width // 128
    piece = slots * chunks
    row_count = n * slots
    blocks = vocab // largest_block(vocab, 1600, 16)
    lanes = max(128, row_count)
    group = min(n, 32)
    small = jax.ShapeDtypeStruct((1, slots), jnp.float32)
    logprob, entropy = pl.pallas_call(
        functools.partial(kernel, n, blocks),
        out_shape=(small, small),
        in_specs=[
            pl.BlockSpec(memory_space=pl.ANY),
            pl.BlockSpec(memory_space=pl.ANY),
            pl.BlockSpec(memory_space=pl.ANY),
            pl.BlockSpec(memory_space=pltpu.SMEM),
            pl.BlockSpec(memory_space=pltpu.SMEM),
        ],
        out_specs=(pl.BlockSpec(memory_space=pltpu.VMEM),) * 2,
        scratch_shapes=[
            pltpu.VMEM((slots, width), jnp.bfloat16),
            pltpu.VMEM((chunks, 128), jnp.float32),
            pltpu.VMEM((vocab, width), jnp.bfloat16),
            pltpu.VMEM((n * piece, 128), jnp.bfloat16),
            pltpu.VMEM((group, slots, chunks, 128), jnp.float32),
            pltpu.VMEM((row_count, width), jnp.bfloat16),
            pltpu.VMEM((vocab, row_count), jnp.float32),
            pltpu.VMEM((1, lanes), jnp.int32),
            pltpu.VMEM((n, 1, lanes), jnp.int32),
            pltpu.VMEM((n, 1, 128), jnp.float32),
            pltpu.VMEM((n, 1, 128), jnp.float32),
            pltpu.SemaphoreType.DMA((2,)),
            pltpu.SemaphoreType.DMA((blocks,)),
            pltpu.SemaphoreType.DMA,
            pltpu.SemaphoreType.DMA((n,)),
            pltpu.SemaphoreType.DMA,
            pltpu.SemaphoreType.DMA,
            pltpu.SemaphoreType.DMA,
            pltpu.SemaphoreType.DMA,
        ],
        compiler_params=pltpu.CompilerParams(
            collective_id=0, has_side_effects=True, vmem_limit_bytes=48 * 2**20
        ),
        name="head_stats",
    )(hidden, norm_gain.reshape(chunks, 128), head_weight, targets, spans)
    return logprob.reshape(slots), entropy.reshape(slots)


def solution(mesh):
    return jax.shard_map(
        functools.partial(local, mesh.shape["blk"]),
        mesh=mesh,
        in_specs=(P("blk", None), P(), P("blk", None), P("blk"), P("blk", None)),
        out_specs=(P("blk"), P("blk")),
        check_vma=False,
    )
```

```python
import functools

import jax
import jax.numpy as jnp
from jax import lax
from jax.experimental import pallas as pl
from jax.experimental.pallas import tpu as pltpu
from jax.sharding import PartitionSpec as P

epsilon = 1e-06
MESH = pl.DeviceIdType.MESH


def largest_block(count, limit, step):
    sizes = [size for size in range(step, min(count, limit) + 1, step) if count % size == 0]
    return max(sizes) if sizes else count


def layout_of(n):
    size = 8 if n % 8 == 0 else n
    return size, n // size


def kernel(
    n, blocks, hidden_ref, gain_ref, weight_ref, targets_ref, spans_ref, out_ref,
    hid, gain, weight, small_targets, small_spans, rows, wide, operand, logits,
    all_targets, message, inbox, onward, last, load_sem, weight_sem,
    row_send, high_recv, near_recv, far_recv, target_send, target_high, target_near,
    stat_send, stat_recv, last_send, last_recv,
):
    me = lax.axis_index("blk")
    slots, width = hid.shape
    chunks = width // 128
    piece = slots * chunks
    row_count = n * slots
    block = weight.shape[0] // blocks
    near_size, high_size = layout_of(n)
    near = lax.rem(me, near_size)
    high = me // near_size
    core = lax.rem(near, 2)
    plane = near // 2
    planes = near_size // 2

    loads = [
        pltpu.make_async_copy(source, target, load_sem.at[index])
        for index, (source, target) in enumerate(
            zip(
                (hidden_ref, gain_ref, targets_ref, spans_ref),
                (hid, gain, small_targets, small_spans),
            )
        )
    ]
    for load in loads:
        load.start()

    def weight_copy(index):
        where = pl.ds(index * block, block)
        return pltpu.make_async_copy(weight_ref.at[where], weight.at[where], weight_sem.at[index])

    for index in range(blocks):
        weight_copy(index).start()

    def device(high_index, near_index):
        return (high_index * near_size + near_index,)

    def other_high(step):
        return lax.rem(high + step, high_size)

    def other_near(step):
        return lax.rem(near + step, near_size)

    def other_plane(step):
        return lax.rem(plane + step, planes) * 2

    barrier = pltpu.get_barrier_semaphore()

    @pl.loop(1, high_size)
    def _(step):
        pl.semaphore_signal(
            barrier, inc=1, device_id=device(other_high(step), near), device_id_type=MESH
        )

    for step in range(1, near_size):
        pl.semaphore_signal(
            barrier, inc=1, device_id=device(high, other_near(step)), device_id_type=MESH
        )

    loads[0].wait()
    values = hid[...].astype(jnp.float32)
    meansq = jnp.mean(values * values, axis=-1, keepdims=True)
    values = values * lax.rsqrt(meansq + epsilon)
    mine = wide.at[0]
    for chunk in range(chunks):
        mine[:, chunk, :] = values[:, chunk * 128 : (chunk + 1) * 128]
    loads[1].wait()
    normed = (mine[...] * gain[...][None]).astype(jnp.bfloat16)
    rows[near, high] = normed.reshape(piece, 128)

    loads[2].wait()
    loads[3].wait()
    lanes = lax.broadcasted_iota(jnp.int32, (1, all_targets.shape[-1]), 1)
    spread = jnp.zeros(lanes.shape, jnp.int32)
    for slot in range(slots):
        place = slot * n + near * high_size + high
        spread = jnp.where(lanes == place, small_targets[slot], spread)
    all_targets[near, high] = spread

    pl.semaphore_wait(barrier, high_size + near_size - 2)

    def remote(source, target, send_sem, recv_sem, device_id):
        return pltpu.make_async_remote_copy(
            src_ref=source,
            dst_ref=target,
            send_sem=send_sem,
            recv_sem=recv_sem,
            device_id=device_id,
            device_id_type=MESH,
        )

    def drain(ref, semaphore):
        pltpu.make_async_copy(ref, ref, semaphore).wait()

    @pl.loop(1, high_size)
    def _(step):
        view = rows.at[near, high]
        remote(view, view, row_send, high_recv, device(other_high(step), near)).start()

    @pl.loop(1, high_size)
    def _(step):
        view = all_targets.at[near, high]
        remote(view, view, target_send, target_high, device(other_high(step), near)).start()

    if high_size > 1:
        drain(rows.at[0, pl.ds(0, high_size - 1)], high_recv)
    own = rows.at[near]
    for step in range(1, planes):
        remote(
            own, own, row_send, near_recv.at[planes - step], device(high, other_plane(step) + core)
        ).start()
    remote(own, own, row_send, near_recv.at[0], device(high, plane * 2 + 1 - core)).start()
    if high_size > 1:
        drain(all_targets.at[0, pl.ds(0, high_size - 1)], target_high)
    own = all_targets.at[near]
    for step in range(1, near_size):
        remote(own, own, target_send, target_near, device(high, other_near(step))).start()
    for step in range(1, planes):
        view = rows.at[other_plane(step) + core]
        remote(view, view, row_send, near_recv.at[step], device(high, near)).wait_recv()
        remote(
            view, view, row_send, far_recv.at[step], device(high, plane * 2 + 1 - core)
        ).start()

    near_view = rows.at[plane * 2 + 1 - core]
    remote(near_view, near_view, row_send, near_recv.at[0], device(high, near)).wait_recv()
    for step in range(1, planes):
        view = rows.at[other_plane(step) + 1 - core]
        remote(view, view, row_send, far_recv.at[step], device(high, near)).wait_recv()

    group = wide.shape[0]

    @pl.loop(0, n // group)
    def _(index):
        if group >= high_size:
            count = group // high_size
            block_rows = rows[pl.ds(index * count, count)]
        else:
            count = high_size // group
            block_rows = rows[index // count, pl.ds(lax.rem(index, count) * group, group)]
        wide[...] = block_rows.astype(jnp.float32).reshape(group, slots, chunks, 128)
        for slot in range(slots):
            place = pl.ds(pl.multiple_of(slot * n + index * group, group), group)
            for chunk in range(chunks):
                operand[place, chunk * 128 : (chunk + 1) * 128] = wide[:, slot, chunk, :].astype(
                    jnp.bfloat16
                )

    def multiply(index):
        weight_copy(index).wait()
        where = pl.ds(index * block, block)
        logits[where, :] = lax.dot_general(
            weight[where, :],
            operand[...],
            (((1,), (1,)), ((), ())),
            preferred_element_type=jnp.float32,
        )

    multiply(0)
    drain(all_targets.at[pl.ds(0, near_size - 1)], target_near)
    wanted = all_targets[...].reshape(n, -1)
    wanted = jnp.sum(wanted, axis=0, keepdims=True)[:, :row_count] - me * weight.shape[0]

    def stats(index):
        found = logits[pl.ds(index * block, block), :]
        column = lax.broadcasted_iota(jnp.int32, found.shape, 0)
        peak = jnp.max(found, axis=0, keepdims=True)
        expon = jnp.exp(found - peak)
        return (
            peak,
            jnp.sum(expon, axis=0, keepdims=True),
            jnp.sum(expon * found, axis=0, keepdims=True),
            jnp.sum(
                jnp.where(column == wanted - index * block, found, 0.0), axis=0, keepdims=True
            ),
        )

    parts = []
    for index in range(blocks):
        if index + 1 < blocks:
            multiply(index + 1)
        parts.append(stats(index))
    peak = functools.reduce(jnp.maximum, [part[0] for part in parts])
    scales = [jnp.exp(part[0] - peak) for part in parts]
    total = sum(part[1] * scale for part, scale in zip(parts, scales))
    moment = sum(part[2] * scale for part, scale in zip(parts, scales))
    picked = sum(part[3] for part in parts)

    def by_slot(item):
        return [item[:, slot * n : (slot + 1) * n] for slot in range(slots)]

    blank = [jnp.zeros((1, n), jnp.float32)] * slots
    packed = jnp.concatenate(
        by_slot(total) + by_slot(moment) + by_slot(picked) + blank
        + by_slot(peak) + by_slot(peak) + blank + blank,
        axis=0,
    )
    fields = packed.shape[0]
    turned = jnp.concatenate([packed.T, jnp.zeros((n, 128 - fields), jnp.float32)], axis=1)
    for index in range(near_size):
        message[index] = turned[index * high_size : (index + 1) * high_size]

    inbox[near] = message[near]
    for step in range(1, near_size):
        remote(
            message.at[other_near(step)], inbox.at[near], stat_send, stat_recv,
            device(high, other_near(step)),
        ).start()
    drain(inbox.at[pl.ds(0, near_size - 1)], stat_recv)

    def merge(arrived, axis):
        peaks = pltpu.roll(arrived, 128 - fields // 2, arrived.ndim - 1)
        top = jnp.max(peaks, axis=axis)
        return jnp.sum(arrived * jnp.exp(peaks - top[None]), axis=axis), top

    arrived = inbox[...]
    merged, _ = merge(arrived, 0)
    lane = lax.broadcasted_iota(jnp.int32, merged.shape, 1)
    merged = jnp.where(lane < fields // 2, merged, jnp.max(arrived, axis=0))
    onward[...] = merged.reshape(high_size, 1, 128)
    last[high] = onward[high]

    @pl.loop(1, high_size)
    def _(step):
        remote(
            onward.at[other_high(step)], last.at[high], last_send, last_recv,
            device(other_high(step), near),
        ).start()

    if high_size > 1:
        drain(last.at[pl.ds(0, high_size - 1)], last_recv)
    merged, top = merge(last[...].reshape(high_size, 128), 0)
    merged, top = merged[None], top[None]
    lse = top + jnp.log(merged)
    expected = pltpu.roll(merged, 128 - slots, 1) / merged
    chosen = pltpu.roll(merged, 128 - 2 * slots, 1)
    slot_ids = lax.broadcasted_iota(jnp.int32, (1, 128), 1)
    scored = (slot_ids >= small_spans[0, 0]) & (slot_ids < small_spans[0, 1])
    out_ref[0:1, :] = jnp.where(scored, chosen - lse, 0.0)
    out_ref[1:2, :] = jnp.where(scored, lse - expected, 0.0)

    for step in range(2 * planes - 1):
        drain(rows.at[0], row_send)
    if high_size > 1:
        drain(rows.at[0, pl.ds(0, high_size - 1)], row_send)
        drain(all_targets.at[0, pl.ds(0, high_size - 1)], target_send)
        drain(last.at[pl.ds(0, high_size - 1)], last_send)
    drain(all_targets.at[pl.ds(0, near_size - 1)], target_send)
    drain(inbox.at[pl.ds(0, near_size - 1)], stat_send)


def local(n, hidden, norm_gain, head_weight, targets, spans):
    slots, width = hidden.shape
    vocab = head_weight.shape[0]
    chunks = width // 128
    piece = slots * chunks
    row_count = n * slots
    blocks = vocab // largest_block(vocab, 800, 16)
    lanes = max(128, row_count)
    near_size, high_size = layout_of(n)
    group = min(n, 32)
    out = pl.pallas_call(
        functools.partial(kernel, n, blocks),
        out_shape=jax.ShapeDtypeStruct((2, 128), jnp.float32),
        in_specs=[pl.BlockSpec(memory_space=pltpu.HBM)] * 5,
        out_specs=pl.BlockSpec(memory_space=pltpu.VMEM),
        scratch_shapes=[
            pltpu.VMEM((slots, width), jnp.bfloat16),
            pltpu.VMEM((chunks, 128), jnp.float32),
            pltpu.VMEM((vocab, width), jnp.bfloat16),
            pltpu.SMEM(targets.shape, jnp.int32),
            pltpu.SMEM(spans.shape, jnp.int32),
            pltpu.VMEM((near_size, high_size, piece, 128), jnp.bfloat16),
            pltpu.VMEM((group, slots, chunks, 128), jnp.float32),
            pltpu.VMEM((row_count, width), jnp.bfloat16),
            pltpu.VMEM((vocab, row_count), jnp.float32),
            pltpu.VMEM((near_size, high_size, 1, lanes), jnp.int32),
            pltpu.VMEM((near_size, high_size, 128), jnp.float32),
            pltpu.VMEM((near_size, high_size, 128), jnp.float32),
            pltpu.VMEM((high_size, 1, 128), jnp.float32),
            pltpu.VMEM((high_size, 1, 128), jnp.float32),
            pltpu.SemaphoreType.DMA((4,)),
            pltpu.SemaphoreType.DMA((blocks,)),
            pltpu.SemaphoreType.DMA,
            pltpu.SemaphoreType.DMA,
            pltpu.SemaphoreType.DMA((near_size // 2,)),
            pltpu.SemaphoreType.DMA((near_size // 2,)),
            pltpu.SemaphoreType.DMA,
            pltpu.SemaphoreType.DMA,
            pltpu.SemaphoreType.DMA,
            pltpu.SemaphoreType.DMA,
            pltpu.SemaphoreType.DMA,
            pltpu.SemaphoreType.DMA,
            pltpu.SemaphoreType.DMA,
        ],
        compiler_params=pltpu.CompilerParams(
            collective_id=0, has_side_effects=True, vmem_limit_bytes=60 * 2**20
        ),
        name="head_stats",
    )(hidden, norm_gain.reshape(chunks, 128), head_weight, targets, spans)
    return out[0, :slots], out[1, :slots]


def solution(mesh):
    return jax.shard_map(
        functools.partial(local, mesh.shape["blk"]),
        mesh=mesh,
        in_specs=(P("blk", None), P(), P("blk", None), P("blk"), P("blk", None)),
        out_specs=(P("blk"), P("blk")),
        check_vma=False,
    )
```

```python
import functools

import jax
import jax.numpy as jnp
from jax import lax
from jax.experimental import pallas as pl
from jax.experimental.pallas import tpu as pltpu
from jax.sharding import PartitionSpec as P

epsilon = 1e-06
MESH = pl.DeviceIdType.MESH


def largest_block(count, limit, step):
    sizes = [size for size in range(step, min(count, limit) + 1, step) if count % size == 0]
    return max(sizes) if sizes else count


def layout_of(n):
    size = 8 if n % 8 == 0 else n
    return size, n // size


def kernel(
    n, blocks, hidden_ref, gain_ref, weight_ref, targets_ref, spans_ref, out_ref,
    hid, gain, weight, small_targets, small_spans, rows, wide, operand,
    all_targets, message, inbox, load_sem, weight_sem,
    row_send, high_recv, near_recv, far_recv, target_send, target_high, target_near,
    stat_send, stat_recv,
):
    me = lax.axis_index("blk")
    slots, width = hid.shape
    chunks = width // 128
    piece = slots * chunks
    row_count = n * slots
    block = weight.shape[0] // blocks
    near_size, high_size = layout_of(n)
    near = lax.rem(me, near_size)
    high = me // near_size
    core = lax.rem(near, 2)
    plane = near // 2
    planes = near_size // 2

    loads = [
        pltpu.make_async_copy(source, target, load_sem.at[index])
        for index, (source, target) in enumerate(
            zip(
                (hidden_ref, gain_ref, targets_ref, spans_ref),
                (hid, gain, small_targets, small_spans),
            )
        )
    ]
    for load in loads:
        load.start()

    def weight_copy(index):
        where = pl.ds(index * block, block)
        return pltpu.make_async_copy(weight_ref.at[where], weight.at[where], weight_sem.at[index])

    for index in range(blocks):
        weight_copy(index).start()

    def device(high_index, near_index):
        return (high_index * near_size + near_index,)

    def other_high(step):
        return lax.rem(high + step, high_size)

    def other_near(step):
        return lax.rem(near + step, near_size)

    def other_plane(step):
        return lax.rem(plane + step, planes) * 2

    barrier = pltpu.get_barrier_semaphore()

    @pl.loop(1, n)
    def _(step):
        pl.semaphore_signal(barrier, inc=1, device_id=(lax.rem(me + step, n),), device_id_type=MESH)

    loads[0].wait()
    values = hid[...].astype(jnp.float32)
    meansq = jnp.mean(values * values, axis=-1, keepdims=True)
    values = values * lax.rsqrt(meansq + epsilon)
    mine = wide.at[0]
    for chunk in range(chunks):
        mine[:, chunk, :] = values[:, chunk * 128 : (chunk + 1) * 128]
    loads[1].wait()
    normed = (mine[...] * gain[...][None]).astype(jnp.bfloat16)
    rows[near, high] = normed.reshape(piece, 128)

    loads[2].wait()
    loads[3].wait()
    lanes = lax.broadcasted_iota(jnp.int32, (1, all_targets.shape[-1]), 1)
    spread = jnp.zeros(lanes.shape, jnp.int32)
    for slot in range(slots):
        place = slot * n + near * high_size + high
        spread = jnp.where(lanes == place, small_targets[slot], spread)
    all_targets[near, high] = spread

    pl.semaphore_wait(barrier, n - 1)

    def remote(source, target, send_sem, recv_sem, device_id):
        return pltpu.make_async_remote_copy(
            src_ref=source,
            dst_ref=target,
            send_sem=send_sem,
            recv_sem=recv_sem,
            device_id=device_id,
            device_id_type=MESH,
        )

    def drain(ref, semaphore):
        pltpu.make_async_copy(ref, ref, semaphore).wait()

    @pl.loop(1, high_size)
    def _(step):
        view = rows.at[near, high]
        remote(view, view, row_send, high_recv, device(other_high(step), near)).start()

    @pl.loop(1, high_size)
    def _(step):
        view = all_targets.at[near, high]
        remote(view, view, target_send, target_high, device(other_high(step), near)).start()

    if high_size > 1:
        drain(rows.at[0, pl.ds(0, high_size - 1)], high_recv)
    own = rows.at[near]
    for step in range(1, planes):
        remote(
            own, own, row_send, near_recv.at[planes - step], device(high, other_plane(step) + core)
        ).start()
    remote(own, own, row_send, near_recv.at[0], device(high, plane * 2 + 1 - core)).start()
    if high_size > 1:
        drain(all_targets.at[0, pl.ds(0, high_size - 1)], target_high)
    own = all_targets.at[near]
    for step in range(1, near_size):
        remote(own, own, target_send, target_near, device(high, other_near(step))).start()
    for step in range(1, planes):
        view = rows.at[other_plane(step) + core]
        remote(view, view, row_send, near_recv.at[step], device(high, near)).wait_recv()
        remote(
            view, view, row_send, far_recv.at[step], device(high, plane * 2 + 1 - core)
        ).start()

    near_view = rows.at[plane * 2 + 1 - core]
    remote(near_view, near_view, row_send, near_recv.at[0], device(high, near)).wait_recv()
    for step in range(1, planes):
        view = rows.at[other_plane(step) + 1 - core]
        remote(view, view, row_send, far_recv.at[step], device(high, near)).wait_recv()

    group = wide.shape[0]

    @pl.loop(0, n // group)
    def _(index):
        if group >= high_size:
            count = group // high_size
            block_rows = rows[pl.ds(index * count, count)]
        else:
            count = high_size // group
            block_rows = rows[index // count, pl.ds(lax.rem(index, count) * group, group)]
        wide[...] = block_rows.astype(jnp.float32).reshape(group, slots, chunks, 128)
        for slot in range(slots):
            place = pl.ds(pl.multiple_of(slot * n + index * group, group), group)
            for chunk in range(chunks):
                operand[place, chunk * 128 : (chunk + 1) * 128] = wide[:, slot, chunk, :].astype(
                    jnp.bfloat16
                )

    drain(all_targets.at[pl.ds(0, near_size - 1)], target_near)
    wanted = all_targets[...].reshape(n, -1)
    wanted = jnp.sum(wanted, axis=0, keepdims=True)[:, :row_count] - me * weight.shape[0]

    def step_block(index, carry):
        weight_copy(index).wait()
        where = pl.ds(pl.multiple_of(index * block, block), block)
        found = lax.dot_general(
            weight[where, :],
            operand[...],
            (((1,), (1,)), ((), ())),
            preferred_element_type=jnp.float32,
        )
        column = lax.broadcasted_iota(jnp.int32, found.shape, 0)
        peak = jnp.maximum(carry[0], jnp.max(found, axis=0, keepdims=True))
        scale = jnp.exp(carry[0] - peak)
        expon = jnp.exp(found - peak)
        chosen = jnp.where(column == wanted - index * block, found, 0.0)
        return (
            peak,
            carry[1] * scale + jnp.sum(expon, axis=0, keepdims=True),
            carry[2] * scale + jnp.sum(expon * found, axis=0, keepdims=True),
            carry[3] + jnp.sum(chosen, axis=0, keepdims=True),
        )

    zero = jnp.zeros((1, row_count), jnp.float32)
    peak, total, moment, picked = lax.fori_loop(
        0, blocks, step_block, (jnp.full((1, row_count), -jnp.inf, jnp.float32), zero, zero, zero)
    )

    def by_slot(item):
        return [item[:, slot * n : (slot + 1) * n] for slot in range(slots)]

    blank = [jnp.zeros((1, n), jnp.float32)] * slots
    packed = jnp.concatenate(
        by_slot(total) + by_slot(moment) + by_slot(picked) + blank
        + by_slot(peak) + by_slot(peak) + blank + blank,
        axis=0,
    )
    fields = packed.shape[0]
    turned = jnp.concatenate([packed.T, jnp.zeros((n, 128 - fields), jnp.float32)], axis=1)
    message[...] = turned.reshape(n, 1, 128)
    mine_at = near * high_size + high
    inbox[mine_at] = message[mine_at]

    @pl.loop(1, n)
    def _(step):
        other = lax.rem(me + step, n)
        remote(
            message.at[lax.rem(other, near_size) * high_size + other // near_size],
            inbox.at[mine_at], stat_send, stat_recv, (other,),
        ).start()

    drain(inbox.at[pl.ds(0, n - 1)], stat_recv)
    arrived = inbox[...].reshape(n, 128)
    peaks = pltpu.roll(arrived, 128 - fields // 2, 1)
    top = jnp.max(peaks, axis=0, keepdims=True)
    merged = jnp.sum(arrived * jnp.exp(peaks - top), axis=0, keepdims=True)
    lse = top + jnp.log(merged)
    expected = pltpu.roll(merged, 128 - slots, 1) / merged
    chosen = pltpu.roll(merged, 128 - 2 * slots, 1)
    slot_ids = lax.broadcasted_iota(jnp.int32, (1, 128), 1)
    scored = (slot_ids >= small_spans[0, 0]) & (slot_ids < small_spans[0, 1])
    out_ref[0:1, :] = jnp.where(scored, chosen - lse, 0.0)
    out_ref[1:2, :] = jnp.where(scored, lse - expected, 0.0)

    for step in range(2 * planes - 1):
        drain(rows.at[0], row_send)
    if high_size > 1:
        drain(rows.at[0, pl.ds(0, high_size - 1)], row_send)
        drain(all_targets.at[0, pl.ds(0, high_size - 1)], target_send)
    drain(all_targets.at[pl.ds(0, near_size - 1)], target_send)
    drain(inbox.at[pl.ds(0, n - 1)], stat_send)


def local(n, hidden, norm_gain, head_weight, targets, spans):
    slots, width = hidden.shape
    vocab = head_weight.shape[0]
    chunks = width // 128
    piece = slots * chunks
    row_count = n * slots
    blocks = vocab // largest_block(vocab, 640, 16)
    lanes = max(128, row_count)
    near_size, high_size = layout_of(n)
    group = min(n, 32)
    out = pl.pallas_call(
        functools.partial(kernel, n, blocks),
        out_shape=jax.ShapeDtypeStruct((2, 128), jnp.float32),
        in_specs=[pl.BlockSpec(memory_space=pltpu.HBM)] * 5,
        out_specs=pl.BlockSpec(memory_space=pltpu.VMEM),
        scratch_shapes=[
            pltpu.VMEM((slots, width), jnp.bfloat16),
            pltpu.VMEM((chunks, 128), jnp.float32),
            pltpu.VMEM((vocab, width), jnp.bfloat16),
            pltpu.SMEM(targets.shape, jnp.int32),
            pltpu.SMEM(spans.shape, jnp.int32),
            pltpu.VMEM((near_size, high_size, piece, 128), jnp.bfloat16),
            pltpu.VMEM((group, slots, chunks, 128), jnp.float32),
            pltpu.VMEM((row_count, width), jnp.bfloat16),
            pltpu.VMEM((near_size, high_size, 1, lanes), jnp.int32),
            pltpu.VMEM((n, 1, 128), jnp.float32),
            pltpu.VMEM((n, 1, 128), jnp.float32),
            pltpu.SemaphoreType.DMA((4,)),
            pltpu.SemaphoreType.DMA((blocks,)),
            pltpu.SemaphoreType.DMA,
            pltpu.SemaphoreType.DMA,
            pltpu.SemaphoreType.DMA((near_size // 2,)),
            pltpu.SemaphoreType.DMA((near_size // 2,)),
            pltpu.SemaphoreType.DMA,
            pltpu.SemaphoreType.DMA,
            pltpu.SemaphoreType.DMA,
            pltpu.SemaphoreType.DMA,
            pltpu.SemaphoreType.DMA,
        ],
        compiler_params=pltpu.CompilerParams(
            collective_id=0, has_side_effects=True, vmem_limit_bytes=60 * 2**20
        ),
        name="head_stats",
    )(hidden, norm_gain.reshape(chunks, 128), head_weight, targets, spans)
    return out[0, :slots], out[1, :slots]


def solution(mesh):
    return jax.shard_map(
        functools.partial(local, mesh.shape["blk"]),
        mesh=mesh,
        in_specs=(P("blk", None), P(), P("blk", None), P("blk"), P("blk", None)),
        out_specs=(P("blk"), P("blk")),
        check_vma=False,
    )
```

```python
import functools

import jax
import jax.numpy as jnp
from jax import lax
from jax.experimental import pallas as pl
from jax.experimental.pallas import tpu as pltpu
from jax.sharding import PartitionSpec as P

epsilon = 1e-06
MESH = pl.DeviceIdType.MESH


def largest_block(count, limit, step):
    sizes = [size for size in range(step, min(count, limit) + 1, step) if count % size == 0]
    return max(sizes) if sizes else count


def layout_of(n):
    size = 8 if n % 8 == 0 else n
    return size, n // size


def kernel(
    n, blocks, hidden_ref, gain_ref, weight_ref, targets_ref, spans_ref, out_ref,
    hid, gain, weight, small_targets, small_spans, rows, wide, operand,
    all_targets, message, inbox, load_sem, weight_sem,
    row_send, high_recv, near_recv, far_recv, target_send, target_high, target_near,
    stat_send, stat_recv,
):
    me = lax.axis_index("blk")
    slots, width = hid.shape
    chunks = width // 128
    piece = slots * chunks
    row_count = n * slots
    block = weight.shape[0] // blocks
    near_size, high_size = layout_of(n)
    near = lax.rem(me, near_size)
    high = me // near_size
    core = lax.rem(near, 2)
    plane = near // 2
    planes = near_size // 2

    loads = [
        pltpu.make_async_copy(source, target, load_sem.at[index])
        for index, (source, target) in enumerate(
            zip(
                (hidden_ref, gain_ref, targets_ref, spans_ref),
                (hid, gain, small_targets, small_spans),
            )
        )
    ]
    for load in loads:
        load.start()

    def weight_copy(index):
        where = pl.ds(index * block, block)
        return pltpu.make_async_copy(weight_ref.at[where], weight.at[where], weight_sem.at[index])

    for index in range(blocks):
        weight_copy(index).start()

    def device(high_index, near_index):
        return (high_index * near_size + near_index,)

    def other_high(step):
        return lax.rem(high + step, high_size)

    def other_near(step):
        return lax.rem(near + step, near_size)

    def other_plane(step):
        return lax.rem(plane + step, planes) * 2

    barrier = pltpu.get_barrier_semaphore()

    nears = [other_near(step) for step in range(near_size)]

    def greet(high_index, near_index):
        pl.semaphore_signal(
            barrier, inc=1, device_id=device(high_index, near_index), device_id_type=MESH
        )

    for near_index in nears[1:]:
        greet(high, near_index)

    @pl.loop(1, high_size)
    def _(step):
        for near_index in nears:
            greet(other_high(step), near_index)

    loads[0].wait()
    values = hid[...].astype(jnp.float32)
    meansq = jnp.mean(values * values, axis=-1, keepdims=True)
    values = values * lax.rsqrt(meansq + epsilon)
    mine = wide.at[0]
    for chunk in range(chunks):
        mine[:, chunk, :] = values[:, chunk * 128 : (chunk + 1) * 128]
    loads[1].wait()
    normed = (mine[...] * gain[...][None]).astype(jnp.bfloat16)
    rows[near, high] = normed.reshape(piece, 128)

    loads[2].wait()
    loads[3].wait()
    lanes = lax.broadcasted_iota(jnp.int32, (1, all_targets.shape[-1]), 1)
    spread = jnp.zeros(lanes.shape, jnp.int32)
    for slot in range(slots):
        place = slot * n + near * high_size + high
        spread = jnp.where(lanes == place, small_targets[slot], spread)
    all_targets[near, high] = spread

    pl.semaphore_wait(barrier, n - 1)

    def remote(source, target, send_sem, recv_sem, device_id):
        return pltpu.make_async_remote_copy(
            src_ref=source,
            dst_ref=target,
            send_sem=send_sem,
            recv_sem=recv_sem,
            device_id=device_id,
            device_id_type=MESH,
        )

    def drain(ref, semaphore):
        pltpu.make_async_copy(ref, ref, semaphore).wait()

    def send_row(high_index, turn):
        view = rows.at[near, high]
        remote(
            view, view, row_send, near_recv.at[(planes - turn) % planes],
            device(high_index, other_plane(turn) + core),
        ).start()

    @pl.loop(1, high_size)
    def _(step):
        for turn in range(planes):
            send_row(other_high(step), turn)

    for turn in range(1, planes):
        send_row(high, turn)

    @pl.loop(1, high_size)
    def _(step):
        view = all_targets.at[near, high]
        remote(view, view, target_send, target_high, device(other_high(step), near)).start()

    if high_size > 1:
        drain(all_targets.at[0, pl.ds(0, high_size - 1)], target_high)
    own = all_targets.at[near]

    @pl.loop(1, near_size)
    def _(step):
        remote(own, own, target_send, target_near, device(high, other_near(step))).start()

    mate = device(high, plane * 2 + 1 - core)
    if high_size > 1:
        drain(rows.at[0, pl.ds(0, high_size - 1)], near_recv.at[0])
    for step in range(planes):
        view = rows.at[other_plane(step) + core]
        if step > 0:
            drain(view, near_recv.at[step])
        remote(view, view, row_send, far_recv.at[step], mate).start()
    for step in range(planes):
        drain(rows.at[other_plane(step) + 1 - core], far_recv.at[step])

    group = wide.shape[0]

    @pl.loop(0, n // group)
    def _(index):
        if group >= high_size:
            count = group // high_size
            block_rows = rows[pl.ds(index * count, count)]
        else:
            count = high_size // group
            block_rows = rows[index // count, pl.ds(lax.rem(index, count) * group, group)]
        wide[...] = block_rows.astype(jnp.float32).reshape(group, slots, chunks, 128)
        for slot in range(slots):
            place = pl.ds(pl.multiple_of(slot * n + index * group, group), group)
            for chunk in range(chunks):
                operand[place, chunk * 128 : (chunk + 1) * 128] = wide[:, slot, chunk, :].astype(
                    jnp.bfloat16
                )

    drain(all_targets.at[pl.ds(0, near_size - 1)], target_near)
    wanted = all_targets[...].reshape(n, -1)
    wanted = jnp.sum(wanted, axis=0, keepdims=True)[:, :row_count] - me * weight.shape[0]

    def step_block(index, carry):
        weight_copy(index).wait()
        where = pl.ds(pl.multiple_of(index * block, block), block)
        found = lax.dot_general(
            weight[where, :],
            operand[...],
            (((1,), (1,)), ((), ())),
            preferred_element_type=jnp.float32,
        )
        column = lax.broadcasted_iota(jnp.int32, found.shape, 0)
        peak = jnp.maximum(carry[0], jnp.max(found, axis=0, keepdims=True))
        scale = jnp.exp(carry[0] - peak)
        expon = jnp.exp(found - peak)
        chosen = jnp.where(column == wanted - index * block, found, 0.0)
        return (
            peak,
            carry[1] * scale + jnp.sum(expon, axis=0, keepdims=True),
            carry[2] * scale + jnp.sum(expon * found, axis=0, keepdims=True),
            carry[3] + jnp.sum(chosen, axis=0, keepdims=True),
        )

    zero = jnp.zeros((1, row_count), jnp.float32)
    peak, total, moment, picked = lax.fori_loop(
        0, blocks, step_block, (jnp.full((1, row_count), -jnp.inf, jnp.float32), zero, zero, zero)
    )

    def by_slot(item):
        return [item[:, slot * n : (slot + 1) * n] for slot in range(slots)]

    blank = [jnp.zeros((1, n), jnp.float32)] * slots
    packed = jnp.concatenate(
        by_slot(total) + by_slot(moment) + by_slot(picked) + blank
        + by_slot(peak) + by_slot(peak) + blank + blank,
        axis=0,
    )
    fields = packed.shape[0]
    turned = jnp.concatenate([packed.T, jnp.zeros((n, 128 - fields), jnp.float32)], axis=1)
    message[...] = turned.reshape(n, 1, 128)
    mine_at = near * high_size + high
    inbox[mine_at] = message[mine_at]

    def send_stats(high_index, near_index):
        remote(
            message.at[near_index * high_size + high_index], inbox.at[mine_at],
            stat_send, stat_recv, device(high_index, near_index),
        ).start()

    @pl.loop(1, high_size)
    def _(step):
        for near_index in nears:
            send_stats(other_high(step), near_index)

    for near_index in nears[1:]:
        send_stats(high, near_index)

    drain(inbox.at[pl.ds(0, n - 1)], stat_recv)
    arrived = inbox[...].reshape(n, 128)
    peaks = pltpu.roll(arrived, 128 - fields // 2, 1)
    top = jnp.max(peaks, axis=0, keepdims=True)
    merged = jnp.sum(arrived * jnp.exp(peaks - top), axis=0, keepdims=True)
    lse = top + jnp.log(merged)
    expected = pltpu.roll(merged, 128 - slots, 1) / merged
    chosen = pltpu.roll(merged, 128 - 2 * slots, 1)
    slot_ids = lax.broadcasted_iota(jnp.int32, (1, 128), 1)
    scored = (slot_ids >= small_spans[0, 0]) & (slot_ids < small_spans[0, 1])
    out_ref[0:1, :] = jnp.where(scored, chosen - lse, 0.0)
    out_ref[1:2, :] = jnp.where(scored, lse - expected, 0.0)

    for step in range(2 * planes - 1):
        drain(rows.at[0], row_send)
    if high_size > 1:
        drain(rows.at[0, pl.ds(0, high_size - 1)], row_send)
        drain(all_targets.at[0, pl.ds(0, high_size - 1)], target_send)
    drain(all_targets.at[pl.ds(0, near_size - 1)], target_send)
    drain(inbox.at[pl.ds(0, n - 1)], stat_send)


def local(n, hidden, norm_gain, head_weight, targets, spans):
    slots, width = hidden.shape
    vocab = head_weight.shape[0]
    chunks = width // 128
    piece = slots * chunks
    row_count = n * slots
    blocks = vocab // largest_block(vocab, 1600, 16)
    lanes = max(128, row_count)
    near_size, high_size = layout_of(n)
    group = min(n, 32)
    out = pl.pallas_call(
        functools.partial(kernel, n, blocks),
        out_shape=jax.ShapeDtypeStruct((2, 128), jnp.float32),
        in_specs=[pl.BlockSpec(memory_space=pltpu.HBM)] * 5,
        out_specs=pl.BlockSpec(memory_space=pltpu.VMEM),
        scratch_shapes=[
            pltpu.VMEM((slots, width), jnp.bfloat16),
            pltpu.VMEM((chunks, 128), jnp.float32),
            pltpu.VMEM((vocab, width), jnp.bfloat16),
            pltpu.SMEM(targets.shape, jnp.int32),
            pltpu.SMEM(spans.shape, jnp.int32),
            pltpu.VMEM((near_size, high_size, piece, 128), jnp.bfloat16),
            pltpu.VMEM((group, slots, chunks, 128), jnp.float32),
            pltpu.VMEM((row_count, width), jnp.bfloat16),
            pltpu.VMEM((near_size, high_size, 1, lanes), jnp.int32),
            pltpu.VMEM((n, 1, 128), jnp.float32),
            pltpu.VMEM((n, 1, 128), jnp.float32),
            pltpu.SemaphoreType.DMA((4,)),
            pltpu.SemaphoreType.DMA((blocks,)),
            pltpu.SemaphoreType.DMA,
            pltpu.SemaphoreType.DMA,
            pltpu.SemaphoreType.DMA((near_size // 2,)),
            pltpu.SemaphoreType.DMA((near_size // 2,)),
            pltpu.SemaphoreType.DMA,
            pltpu.SemaphoreType.DMA,
            pltpu.SemaphoreType.DMA,
            pltpu.SemaphoreType.DMA,
            pltpu.SemaphoreType.DMA,
        ],
        compiler_params=pltpu.CompilerParams(
            collective_id=0, has_side_effects=True, vmem_limit_bytes=60 * 2**20
        ),
        name="head_stats",
    )(hidden, norm_gain.reshape(chunks, 128), head_weight, targets, spans)
    return out[0, :slots], out[1, :slots]


def solution(mesh):
    return jax.shard_map(
        functools.partial(local, mesh.shape["blk"]),
        mesh=mesh,
        in_specs=(P("blk", None), P(), P("blk", None), P("blk"), P("blk", None)),
        out_specs=(P("blk"), P("blk")),
        check_vma=False,
    )
```

```python
import functools

import jax
import jax.numpy as jnp
from jax import lax
from jax.experimental import pallas as pl
from jax.experimental.pallas import tpu as pltpu
from jax.sharding import PartitionSpec as P

epsilon = 1e-06
MESH = pl.DeviceIdType.MESH


def largest_block(count, limit, step):
    sizes = [size for size in range(step, min(count, limit) + 1, step) if count % size == 0]
    return max(sizes) if sizes else count


def layout_of(n):
    size = 8 if n % 8 == 0 else n
    return size, n // size


def kernel(
    n, blocks, hidden_ref, gain_ref, weight_ref, targets_ref, spans_ref, logprob_ref, entropy_ref,
    hid, gain, weight, small_targets, small_spans, rows, wide, operand,
    all_targets, message, inbox, load_sem, weight_sem,
    row_send, high_recv, near_recv, far_recv, target_send, target_high, target_near,
    stat_send, stat_recv,
):
    me = lax.axis_index("blk")
    slots, width = hid.shape
    chunks = width // 128
    piece = slots * chunks
    row_count = n * slots
    block = weight.shape[0] // blocks
    near_size, high_size = layout_of(n)
    near = lax.rem(me, near_size)
    high = me // near_size
    core = lax.rem(near, 2)
    plane = near // 2
    planes = near_size // 2

    loads = [
        pltpu.make_async_copy(source, target, load_sem.at[index])
        for index, (source, target) in enumerate(
            zip(
                (hidden_ref, gain_ref, targets_ref, spans_ref),
                (hid, gain, small_targets, small_spans),
            )
        )
    ]
    for load in loads:
        load.start()

    def weight_copy(index):
        where = pl.ds(index * block, block)
        return pltpu.make_async_copy(weight_ref.at[where], weight.at[where], weight_sem.at[index])

    for index in range(blocks):
        weight_copy(index).start()

    def device(high_index, near_index):
        return (high_index * near_size + near_index,)

    def other_high(step):
        return lax.rem(high + step, high_size)

    def other_near(step):
        return lax.rem(near + step, near_size)

    def other_plane(step):
        return lax.rem(plane + step, planes) * 2

    barrier = pltpu.get_barrier_semaphore()

    nears = [other_near(step) for step in range(near_size)]

    def greet(high_index, near_index):
        pl.semaphore_signal(
            barrier, inc=1, device_id=device(high_index, near_index), device_id_type=MESH
        )

    for near_index in nears[1:]:
        greet(high, near_index)

    @pl.loop(1, high_size)
    def _(step):
        for near_index in nears:
            greet(other_high(step), near_index)

    loads[0].wait()
    values = hid[...].astype(jnp.float32)
    meansq = jnp.mean(values * values, axis=-1, keepdims=True)
    values = values * lax.rsqrt(meansq + epsilon)
    mine = wide.at[0]
    for chunk in range(chunks):
        mine[:, chunk, :] = values[:, chunk * 128 : (chunk + 1) * 128]
    loads[1].wait()
    normed = (mine[...] * gain[...][None]).astype(jnp.bfloat16)
    rows[near, high] = normed.reshape(piece, 128)

    loads[2].wait()
    loads[3].wait()
    lanes = lax.broadcasted_iota(jnp.int32, (1, all_targets.shape[-1]), 1)
    spread = jnp.zeros(lanes.shape, jnp.int32)
    for slot in range(slots):
        place = slot * n + near * high_size + high
        spread = jnp.where(lanes == place, small_targets[slot], spread)
    all_targets[near, high] = spread

    pl.semaphore_wait(barrier, n - 1)

    def remote(source, target, send_sem, recv_sem, device_id):
        return pltpu.make_async_remote_copy(
            src_ref=source,
            dst_ref=target,
            send_sem=send_sem,
            recv_sem=recv_sem,
            device_id=device_id,
            device_id_type=MESH,
        )

    def drain(ref, semaphore):
        pltpu.make_async_copy(ref, ref, semaphore).wait()

    def send_row(high_index, turn):
        view = rows.at[near, high]
        remote(
            view, view, row_send, near_recv.at[(planes - turn) % planes],
            device(high_index, other_plane(turn) + core),
        ).start()

    @pl.loop(1, high_size)
    def _(step):
        for turn in range(planes):
            send_row(other_high(step), turn)

    for turn in range(1, planes):
        send_row(high, turn)

    @pl.loop(1, high_size)
    def _(step):
        view = all_targets.at[near, high]
        remote(view, view, target_send, target_high, device(other_high(step), near)).start()

    if high_size > 1:
        drain(all_targets.at[0, pl.ds(0, high_size - 1)], target_high)
    own = all_targets.at[near]

    @pl.loop(1, near_size)
    def _(step):
        remote(own, own, target_send, target_near, device(high, other_near(step))).start()

    mate = device(high, plane * 2 + 1 - core)
    if high_size > 1:
        drain(rows.at[0, pl.ds(0, high_size - 1)], near_recv.at[0])
    for step in range(planes):
        view = rows.at[other_plane(step) + core]
        if step > 0:
            drain(view, near_recv.at[step])
        remote(view, view, row_send, far_recv.at[step], mate).start()
    for step in range(planes):
        drain(rows.at[other_plane(step) + 1 - core], far_recv.at[step])

    group = wide.shape[0]

    @pl.loop(0, n // group)
    def _(index):
        if group >= high_size:
            count = group // high_size
            block_rows = rows[pl.ds(index * count, count)]
        else:
            count = high_size // group
            block_rows = rows[index // count, pl.ds(lax.rem(index, count) * group, group)]
        wide[...] = block_rows.astype(jnp.float32).reshape(group, slots, chunks, 128)
        for slot in range(slots):
            place = pl.ds(pl.multiple_of(slot * n + index * group, group), group)
            for chunk in range(chunks):
                operand[place, chunk * 128 : (chunk + 1) * 128] = wide[:, slot, chunk, :].astype(
                    jnp.bfloat16
                )

    drain(all_targets.at[pl.ds(0, near_size - 1)], target_near)
    wanted = all_targets[...].reshape(n, -1)
    wanted = jnp.sum(wanted, axis=0, keepdims=True)[:, :row_count] - me * weight.shape[0]

    def step_block(index, carry):
        weight_copy(index).wait()
        where = pl.ds(pl.multiple_of(index * block, block), block)
        found = lax.dot_general(
            weight[where, :],
            operand[...],
            (((1,), (1,)), ((), ())),
            preferred_element_type=jnp.float32,
        )
        column = lax.broadcasted_iota(jnp.int32, found.shape, 0)
        peak = jnp.maximum(carry[0], jnp.max(found, axis=0, keepdims=True))
        scale = jnp.exp(carry[0] - peak)
        expon = jnp.exp(found - peak)
        chosen = jnp.where(column == wanted - index * block, found, 0.0)
        return (
            peak,
            carry[1] * scale + jnp.sum(expon, axis=0, keepdims=True),
            carry[2] * scale + jnp.sum(expon * found, axis=0, keepdims=True),
            carry[3] + jnp.sum(chosen, axis=0, keepdims=True),
        )

    zero = jnp.zeros((1, row_count), jnp.float32)
    peak, total, moment, picked = lax.fori_loop(
        0, blocks, step_block, (jnp.full((1, row_count), -jnp.inf, jnp.float32), zero, zero, zero)
    )

    def by_slot(item):
        return [item[:, slot * n : (slot + 1) * n] for slot in range(slots)]

    blank = [jnp.zeros((1, n), jnp.float32)] * slots
    packed = jnp.concatenate(
        by_slot(total) + by_slot(moment) + by_slot(picked) + blank
        + by_slot(peak) + by_slot(peak) + blank + blank,
        axis=0,
    )
    fields = packed.shape[0]
    turned = jnp.concatenate([packed.T, jnp.zeros((n, 128 - fields), jnp.float32)], axis=1)
    message[...] = turned.reshape(n, 1, 128)
    mine_at = near * high_size + high
    inbox[mine_at] = message[mine_at]

    def send_stats(high_index, near_index):
        remote(
            message.at[near_index * high_size + high_index], inbox.at[mine_at],
            stat_send, stat_recv, device(high_index, near_index),
        ).start()

    @pl.loop(1, high_size)
    def _(step):
        for near_index in nears:
            send_stats(other_high(step), near_index)

    for near_index in nears[1:]:
        send_stats(high, near_index)

    drain(inbox.at[pl.ds(0, n - 1)], stat_recv)
    arrived = inbox[...].reshape(n, 128)
    peaks = pltpu.roll(arrived, 128 - fields // 2, 1)
    top = jnp.max(peaks, axis=0, keepdims=True)
    merged = jnp.sum(arrived * jnp.exp(peaks - top), axis=0, keepdims=True)
    lse = top + jnp.log(merged)
    expected = pltpu.roll(merged, 128 - slots, 1) / merged
    chosen = pltpu.roll(merged, 128 - 2 * slots, 1)
    slot_ids = lax.broadcasted_iota(jnp.int32, (1, 128), 1)
    scored = (slot_ids >= small_spans[0, 0]) & (slot_ids < small_spans[0, 1])
    logprob_ref[...] = jnp.where(scored, chosen - lse, 0.0)[:, :slots]
    entropy_ref[...] = jnp.where(scored, lse - expected, 0.0)[:, :slots]

    for step in range(2 * planes - 1):
        drain(rows.at[0], row_send)
    if high_size > 1:
        drain(rows.at[0, pl.ds(0, high_size - 1)], row_send)
        drain(all_targets.at[0, pl.ds(0, high_size - 1)], target_send)
    drain(all_targets.at[pl.ds(0, near_size - 1)], target_send)
    drain(inbox.at[pl.ds(0, n - 1)], stat_send)


def local(n, hidden, norm_gain, head_weight, targets, spans):
    slots, width = hidden.shape
    vocab = head_weight.shape[0]
    chunks = width // 128
    piece = slots * chunks
    row_count = n * slots
    blocks = vocab // largest_block(vocab, 1600, 16)
    lanes = max(128, row_count)
    near_size, high_size = layout_of(n)
    group = min(n, 32)
    small = jax.ShapeDtypeStruct((1, slots), jnp.float32)
    logprob, entropy = pl.pallas_call(
        functools.partial(kernel, n, blocks),
        out_shape=(small, small),
        in_specs=[pl.BlockSpec(memory_space=pltpu.HBM)] * 5,
        out_specs=(pl.BlockSpec(memory_space=pltpu.VMEM),) * 2,
        scratch_shapes=[
            pltpu.VMEM((slots, width), jnp.bfloat16),
            pltpu.VMEM((chunks, 128), jnp.float32),
            pltpu.VMEM((vocab, width), jnp.bfloat16),
            pltpu.SMEM(targets.shape, jnp.int32),
            pltpu.SMEM(spans.shape, jnp.int32),
            pltpu.VMEM((near_size, high_size, piece, 128), jnp.bfloat16),
            pltpu.VMEM((group, slots, chunks, 128), jnp.float32),
            pltpu.VMEM((row_count, width), jnp.bfloat16),
            pltpu.VMEM((near_size, high_size, 1, lanes), jnp.int32),
            pltpu.VMEM((n, 1, 128), jnp.float32),
            pltpu.VMEM((n, 1, 128), jnp.float32),
            pltpu.SemaphoreType.DMA((4,)),
            pltpu.SemaphoreType.DMA((blocks,)),
            pltpu.SemaphoreType.DMA,
            pltpu.SemaphoreType.DMA,
            pltpu.SemaphoreType.DMA((near_size // 2,)),
            pltpu.SemaphoreType.DMA((near_size // 2,)),
            pltpu.SemaphoreType.DMA,
            pltpu.SemaphoreType.DMA,
            pltpu.SemaphoreType.DMA,
            pltpu.SemaphoreType.DMA,
            pltpu.SemaphoreType.DMA,
        ],
        compiler_params=pltpu.CompilerParams(
            collective_id=0, has_side_effects=True, vmem_limit_bytes=60 * 2**20
        ),
        name="head_stats",
    )(hidden, norm_gain.reshape(chunks, 128), head_weight, targets, spans)
    return logprob.reshape(slots), entropy.reshape(slots)


def solution(mesh):
    return jax.shard_map(
        functools.partial(local, mesh.shape["blk"]),
        mesh=mesh,
        in_specs=(P("blk", None), P(), P("blk", None), P("blk"), P("blk", None)),
        out_specs=(P("blk"), P("blk")),
        check_vma=False,
    )
```
